768 devices in a mesh: pop: 48 (over y, z_lo), col: 16 (over z_hi, x, core).
Axes of the slice: x: 4, y: 8, z: 12 (z_hi: 2, z_lo: 6; z = z_hi * 6 + z_lo), core: 2. Of those that a mesh axis runs over, the one named last changes fastest.
Arguments:
- weight: float32 [2304, 16384], P('pop', 'col'), may hold values from -3 to 3
- row_factors: bfloat16 [2304, 4608], P(None, 'pop'), may hold values from -6 to 6
- col_factors: bfloat16 [4608, 16384], P('pop', 'col'), may hold values from -6 to 6
- fitness_ranks: int32 [4608], P('pop'), may hold values from 0 to 4607, each once
Outputs:
- new_weight: float32 [2304, 16384], P('pop', 'col')
The draws below stay inside these ranges and needn't reach their ends.
Inputs may be any that keep to these rules, and one draw needn't show every extreme that they name: fitness_ranks holds each of 0 to 4607 exactly once.
All inputs are finite; a program needn't handle non-finite values.
Results may differ from the reference program's by a relative error of at most 0.0026.
Values may be sent and summed in bfloat16 or wider, within the bound.
No kernel may reach another device: no remote copies, remote signals or barrier semaphores. Data moves between devices by JAX's collectives and lax.ppermute only.
A program may use at most 64 MiB of HBM per device.

```python
import math
import jax
import jax.numpy as jnp

D = 2304
F = 16384
MEMB = 4608


def with_spikes(entries, stream_key, source, target, shards_of, factor):
    owner, partner = [(jnp.arange(entries.shape[position]) // (entries.shape[position] // shards_of)).reshape([-1 if axis == position else 1 for axis in range(entries.ndim)]) for position in (source, target)]
    chosen = jax.random.permutation(stream_key, shards_of)[partner]
    strong = (owner == chosen) | (owner == (partner + shards_of // 2) % shards_of)
    return jnp.where(strong, factor * entries, entries)


def block_levels(key, dims, split, least, top_value):
    def one(position, parts):
        steps = jax.random.uniform(jax.random.fold_in(jax.random.fold_in(key, 6), position), (parts,), jnp.float32, least / len(split), top_value / len(split))
        return jnp.repeat(jnp.exp(steps), dims[position] // parts).reshape((-1,) + (1,) * (len(dims) - position - 1))

    gain = one(*split[0])
    for cut in split[1:]:
        gain = gain * one(*cut)
    return gain


def centred(own_key, extent, deviation, reach, shards=(), held_as=jnp.bfloat16):
    result = deviation * jax.random.normal(own_key, extent, jnp.float32)
    if shards:
        result = result * block_levels(own_key, extent, shards, -0.22, 0.18)
    return jnp.clip(result, -reach, reach).astype(held_as)


def bell_draw_with(key, shape, deviation, bound, cuts, heavy, kind=jnp.bfloat16):
    drawn = deviation * jax.random.normal(key, shape, jnp.float32)
    if cuts:
        drawn = drawn * block_levels(key, shape, cuts, -0.22, 0.18)
    return jnp.clip(with_spikes(drawn, jax.random.fold_in(key, 3), *heavy), -bound, bound).astype(kind)


def setup_inputs(seed: int = 0) -> dict:
    seeds = jax.random.split(jax.random.key(seed), 5)
    return {
        "weight": centred(seeds[0], (D, F), 0.5, 3.0, ((0, 48), (1, 16)), jnp.float32),
        "row_factors": bell_draw_with(seeds[1], (D, MEMB), 1.0, 6.0, ((1, 48),), (1, 0, 48, 3.25)),
        "col_factors": centred(seeds[2], (MEMB, F), 1.0, 6.0, ((0, 48), (1, 16))),
        "fitness_ranks": jax.random.permutation(seeds[3], MEMB).astype(jnp.int32),
    }


def reference(weight, row_factors, col_factors, fitness_ranks):
    shaped = fitness_ranks.astype(jnp.float32) / (MEMB - 1) - 0.5
    scaled = (shaped[:, None] * col_factors.astype(jnp.float32)).astype(jnp.bfloat16)
    update = jnp.dot(row_factors, scaled, preferred_element_type=jnp.float32)
    return weight + 3.0 / math.sqrt(MEMB) * update
```

```python
import math

import jax
import jax.numpy as jnp
from jax import lax
from jax.sharding import Mesh, PartitionSpec as P

YB, ZB = 2, 3


def body(weight, row_factors, col_factors, fitness_ranks):
    ya, yb, za, zb = (lax.axis_size(a) for a in ("ya", "yb", "za", "zb"))
    members = fitness_ranks.shape[0] * ya * yb * za * zb
    rows, cols = weight.shape
    own = fitness_ranks.shape[0]
    near, far = ("yb", "zb"), ("ya", "za")
    shaped = fitness_ranks.astype(jnp.float32) / (members - 1) - 0.5
    scaled = (shaped[:, None] * col_factors.astype(jnp.float32)).astype(jnp.bfloat16)
    part = row_factors.reshape(ya, yb, za, zb, rows, own).transpose(1, 3, 5, 0, 2, 4)
    part = part.reshape(yb * zb, own, ya * za * rows)
    both = jnp.concatenate([jnp.broadcast_to(scaled, (yb * zb, own, cols)), part], axis=2)
    both = lax.all_to_all(both, near, split_axis=0, concat_axis=0, tiled=True)
    both = both.reshape(yb * zb * own, -1)
    partial = lax.dot_general(
        both[:, cols:], both[:, :cols], (((0,), (0,)), ((), ())), preferred_element_type=jnp.float32
    ).astype(jnp.bfloat16)
    partial = partial.reshape(ya * za, rows, cols)
    partial = lax.all_to_all(partial, far, split_axis=0, concat_axis=0, tiled=True)
    update = jnp.sum(partial.astype(jnp.float32), axis=0)
    return weight + 3.0 / math.sqrt(members) * update


def solution(mesh):
    pop, col = mesh.devices.shape
    fine = Mesh(
        mesh.devices.reshape(8 // YB, YB, 6 // ZB, ZB, col), ("ya", "yb", "za", "zb", "col")
    )
    pop = ("ya", "yb", "za", "zb")
    in_specs = (P(pop, "col"), P(None, pop), P(pop, "col"), P(pop))
    out_specs = P(pop, "col")
    return jax.shard_map(body, mesh=fine, in_specs=in_specs, out_specs=out_specs, check_vma=False)
```

```python
import math

import jax
import jax.numpy as jnp
from jax import lax
from jax.sharding import Mesh, PartitionSpec as P

YB, ZB = 2, 3
NEAR = ("y0", "zb")
ALONG = ("y0", "y2", "y1")


def body(weight, row_factors, col_factors, fitness_ranks):
    size = {a: lax.axis_size(a) for a in ("y2", "y1", "y0", "za", "zb")}
    yb, za, zb = size["y0"], size["za"], size["zb"]
    ys = size["y2"] * size["y1"] * yb
    members = fitness_ranks.shape[0] * ys * za * zb
    rows, cols = weight.shape
    own = fitness_ranks.shape[0]
    half = cols // yb
    shaped = fitness_ranks.astype(jnp.float32) / (members - 1) - 0.5
    scaled = (shaped[:, None] * col_factors.astype(jnp.float32)).astype(jnp.bfloat16)
    scaled = scaled.reshape(own, yb, half).transpose(1, 0, 2)
    scaled = jnp.broadcast_to(scaled, (zb, yb, own, half))
    side = lax.axis_index("za") ^ lax.axis_index("core")
    part = row_factors.reshape(size["y2"], size["y1"], yb, za, zb, rows, own)
    part = lax.dynamic_index_in_dim(part, side, 3, False)
    names = ("y2", "y1", "y0", "zb")
    part = part.transpose(3, 5, *[names.index(a) for a in ALONG], 4).reshape(zb, 1, own, ys * rows)
    part = jnp.broadcast_to(part, (zb, yb, own, ys * rows))
    both = jnp.concatenate([scaled, part], axis=3)
    if NEAR[0] == "y0":
        both = both.transpose(1, 0, 2, 3)
    both = both.reshape(zb * yb, own, -1)
    both = lax.all_to_all(both, NEAR, split_axis=0, concat_axis=0, tiled=True)
    both = both.reshape(zb * yb * own, -1)
    factors = both[:, :half]
    part = lax.all_gather(both[:, half:], "core")

    def product(side):
        out = lax.dot_general(
            part[side], factors, (((0,), (0,)), ((), ())), preferred_element_type=jnp.float32
        )
        return out.astype(jnp.bfloat16).reshape(ys, rows, half)

    def reduce_y(block):
        block = lax.all_to_all(block, ALONG, split_axis=0, concat_axis=0, tiled=True)
        block = block.astype(jnp.float32).reshape([size[a] for a in ALONG] + [rows, half])
        where = ALONG.index("y0")
        return jnp.sum(block, axis=tuple(i for i in range(3) if i != where))

    far, near = product(1), product(0)
    far = reduce_y(far).astype(jnp.bfloat16)
    far, near = lax.optimization_barrier((far, near))
    far = lax.ppermute(far, "za", [(0, 1), (1, 0)])
    update = reduce_y(near) + far.astype(jnp.float32)
    update = update.transpose(1, 0, 2).reshape(rows, cols)
    return weight + 3.0 / math.sqrt(members) * update


def solution(mesh):
    pop, col = mesh.devices.shape
    fine = Mesh(
        mesh.devices.reshape(2, 2, YB, 6 // ZB, ZB, col // 2, 2),
        ("y2", "y1", "y0", "za", "zb", "plane", "core"),
    )
    pop, col = ("y2", "y1", "y0", "za", "zb"), ("plane", "core")
    in_specs = (P(pop, col), P(None, pop), P(pop, col), P(pop))
    out_specs = P(pop, col)
    return jax.shard_map(body, mesh=fine, in_specs=in_specs, out_specs=out_specs, check_vma=False)
```

```python
import math

import jax
import jax.numpy as jnp
from jax import lax
from jax.sharding import Mesh, PartitionSpec as P

YB, ZB = 2, 3
NEAR = ("y0", "zb")
PARTNER = (1, 0, 2)
ALONG = ("y1", "y2", "y0")


def body(weight, row_factors, col_factors, fitness_ranks):
    size = {a: lax.axis_size(a) for a in ("y2", "y1", "y0", "za", "zb")}
    yb, za, zb = size["y0"], size["za"], size["zb"]
    ys = size["y2"] * size["y1"] * yb
    members = fitness_ranks.shape[0] * ys * za * zb
    rows, cols = weight.shape
    own = fitness_ranks.shape[0]
    half = cols // yb
    shaped = fitness_ranks.astype(jnp.float32) / (members - 1) - 0.5
    scaled = (shaped[:, None] * col_factors.astype(jnp.float32)).astype(jnp.bfloat16)
    scaled = scaled.reshape(own, yb, half).transpose(1, 0, 2)
    scaled = jnp.broadcast_to(scaled, (zb, yb, own, half))
    here = lax.axis_index("za")
    part = row_factors.reshape(size["y2"], size["y1"], yb, za, zb, rows, own)
    there = lax.dynamic_index_in_dim(part, 1 - here, 3, False)
    there = jnp.stack([there[:, :, :, z] for z in PARTNER], axis=3)
    part = lax.dynamic_index_in_dim(part, here, 3, False)
    part = jnp.where(lax.axis_index("core") == 0, part, there)
    names = ("y2", "y1", "y0", "zb")
    part = part.transpose(3, 5, *[names.index(a) for a in ALONG], 4).reshape(zb, 1, own, ys * rows)
    part = jnp.broadcast_to(part, (zb, yb, own, ys * rows))
    both = jnp.concatenate([scaled, part], axis=3)
    if NEAR[0] == "y0":
        both = both.transpose(1, 0, 2, 3)
    both = both.reshape(zb * yb, own, -1)
    both = lax.all_to_all(both, NEAR, split_axis=0, concat_axis=0, tiled=True)
    both = both.reshape(zb * yb * own, -1)
    factors = both[:, :half]
    part = lax.all_gather(both[:, half:], "core")

    def product(side):
        out = lax.dot_general(
            part[side], factors, (((0,), (0,)), ((), ())), preferred_element_type=jnp.float32
        )
        return out.astype(jnp.bfloat16).reshape(ys, rows, half)

    def reduce_y(block):
        block = lax.all_to_all(block, ALONG, split_axis=0, concat_axis=0, tiled=True)
        block = block.astype(jnp.float32).reshape([size[a] for a in ALONG] + [rows, half])
        where = ALONG.index("y0")
        return jnp.sum(block, axis=tuple(i for i in range(3) if i != where))

    pairs = [(z, zb + PARTNER[z]) for z in range(zb)] + [(zb + PARTNER[z], z) for z in range(zb)]
    far, near = product(1), product(0)
    far = reduce_y(far).astype(jnp.bfloat16)
    far, near = lax.optimization_barrier((far, near))
    far = lax.ppermute(far, ("za", "zb"), pairs)
    update = reduce_y(near) + far.astype(jnp.float32)
    update = update.transpose(1, 0, 2).reshape(rows, cols)
    return weight + 3.0 / math.sqrt(members) * update


def solution(mesh):
    pop, col = mesh.devices.shape
    fine = Mesh(
        mesh.devices.reshape(2, 2, YB, 6 // ZB, ZB, col // 2, 2),
        ("y2", "y1", "y0", "za", "zb", "plane", "core"),
    )
    pop, col = ("y2", "y1", "y0", "za", "zb"), ("plane", "core")
    in_specs = (P(pop, col), P(None, pop), P(pop, col), P(pop))
    out_specs = P(pop, col)
    return jax.shard_map(body, mesh=fine, in_specs=in_specs, out_specs=out_specs, check_vma=False)
```

```python
import math

import jax
import jax.numpy as jnp
from jax import lax
from jax.sharding import Mesh, PartitionSpec as P

YB, ZB = 2, 3
NEAR = ("y0", "zb")
NEAR_ORDER = (1, 2, 0, 4, 5, 3)
PARTNER = (1, 0, 2)
ALONG = ("y1", "y2", "y0")


def body(weight, row_factors, col_factors, fitness_ranks):
    size = {a: lax.axis_size(a) for a in ("y2", "y1", "y0", "za", "zb")}
    yb, za, zb = size["y0"], size["za"], size["zb"]
    ys = size["y2"] * size["y1"] * yb
    members = fitness_ranks.shape[0] * ys * za * zb
    rows, cols = weight.shape
    own = fitness_ranks.shape[0]
    half = cols // yb
    shaped = fitness_ranks.astype(jnp.float32) / (members - 1) - 0.5
    scaled = (shaped[:, None] * col_factors.astype(jnp.float32)).astype(jnp.bfloat16)
    scaled = scaled.reshape(own, yb, half).transpose(1, 0, 2)
    scaled = jnp.broadcast_to(scaled, (zb, yb, own, half))
    here = lax.axis_index("za")
    part = row_factors.reshape(size["y2"], size["y1"], yb, za, zb, rows, own)
    there = lax.dynamic_index_in_dim(part, 1 - here, 3, False)
    there = jnp.stack([there[:, :, :, z] for z in PARTNER], axis=3)
    part = lax.dynamic_index_in_dim(part, here, 3, False)
    part = jnp.where(lax.axis_index("core") == 0, part, there)
    part = jnp.stack([part[:, :, :, z] for z in NEAR_ORDER[:zb]], axis=3)
    names = ("y2", "y1", "y0", "zb")
    part = part.transpose(3, 5, *[names.index(a) for a in ALONG], 4).reshape(zb, 1, own, ys * rows)
    part = jnp.broadcast_to(part, (zb, yb, own, ys * rows))
    both = jnp.concatenate([scaled, part], axis=3)
    if NEAR[0] == "y0":
        both = both.transpose(1, 0, 2, 3)
    both = both.reshape(zb * yb, own, -1)
    both = lax.all_to_all(
        both, NEAR, split_axis=0, concat_axis=0, tiled=True, axis_index_groups=[NEAR_ORDER]
    )
    both = both.reshape(zb * yb * own, -1)
    factors = both[:, :half]
    part = lax.all_gather(both[:, half:], "core")

    def product(side):
        out = lax.dot_general(
            part[side], factors, (((0,), (0,)), ((), ())), preferred_element_type=jnp.float32
        )
        return out.astype(jnp.bfloat16).reshape(ys, rows, half)

    def reduce_y(block):
        block = lax.all_to_all(block, ALONG, split_axis=0, concat_axis=0, tiled=True)
        block = block.astype(jnp.float32).reshape([size[a] for a in ALONG] + [rows, half])
        where = ALONG.index("y0")
        return jnp.sum(block, axis=tuple(i for i in range(3) if i != where))

    pairs = [(z, zb + PARTNER[z]) for z in range(zb)] + [(zb + PARTNER[z], z) for z in range(zb)]
    far, near = product(1), product(0)
    far = reduce_y(far).astype(jnp.bfloat16)
    far, near = lax.optimization_barrier((far, near))
    far = lax.ppermute(far, ("za", "zb"), pairs)
    update = reduce_y(near) + far.astype(jnp.float32)
    update = update.transpose(1, 0, 2).reshape(rows, cols)
    return weight + 3.0 / math.sqrt(members) * update


def solution(mesh):
    pop, col = mesh.devices.shape
    fine = Mesh(
        mesh.devices.reshape(2, 2, YB, 6 // ZB, ZB, col // 2, 2),
        ("y2", "y1", "y0", "za", "zb", "plane", "core"),
    )
    pop, col = ("y2", "y1", "y0", "za", "zb"), ("plane", "core")
    in_specs = (P(pop, col), P(None, pop), P(pop, col), P(pop))
    out_specs = P(pop, col)
    return jax.shard_map(body, mesh=fine, in_specs=in_specs, out_specs=out_specs, check_vma=False)
```

```python
import math

import jax
import jax.numpy as jnp
from jax import lax
from jax.sharding import Mesh, PartitionSpec as P

YB, ZB = 2, 3
NEAR = ("y0", "zb")
NEAR_ORDER = (1, 2, 0, 4, 5, 3)
PARTNER = (1, 0, 2)
ALONG = ("y1", "y2", "y0")


def body(weight, row_factors, col_factors, fitness_ranks):
    size = {a: lax.axis_size(a) for a in ("y2", "y1", "y0", "za", "zb")}
    yb, za, zb = size["y0"], size["za"], size["zb"]
    ys = size["y2"] * size["y1"] * yb
    members = fitness_ranks.shape[0] * ys * za * zb
    rows, cols = weight.shape
    own = fitness_ranks.shape[0]
    half = cols // yb
    shaped = fitness_ranks.astype(jnp.float32) / (members - 1) - 0.5
    scaled = (shaped[:, None] * col_factors.astype(jnp.float32)).astype(jnp.bfloat16)
    scaled = scaled.reshape(own, yb, half).transpose(1, 0, 2)
    scaled = jnp.broadcast_to(scaled, (zb, yb, own, half))
    here = lax.axis_index("za")
    part = row_factors.reshape(size["y2"], size["y1"], yb, za, zb, rows, own)
    there = lax.dynamic_index_in_dim(part, 1 - here, 3, False)
    there = jnp.stack([there[:, :, :, z] for z in PARTNER], axis=3)
    part = lax.dynamic_index_in_dim(part, here, 3, False)
    part = lax.dynamic_index_in_dim(part, lax.axis_index("core"), 1, False)
    packed = []
    there = there.swapaxes(0, 1)
    for rows_of in (there.reshape(ys, zb, rows, own), part.reshape(ys // 2, zb, rows, own)):
        rows_of = jnp.stack([rows_of[:, z] for z in NEAR_ORDER[:zb]])
        packed.append(rows_of.transpose(0, 3, 1, 2).reshape(zb, 1, own, -1))
    part = jnp.concatenate(packed, axis=3)
    part = jnp.broadcast_to(part, (zb, yb, own, part.shape[3]))
    both = jnp.concatenate([scaled, part], axis=3)
    if NEAR[0] == "y0":
        both = both.transpose(1, 0, 2, 3)
    both = both.reshape(zb * yb, own, -1)
    both = lax.all_to_all(
        both, NEAR, split_axis=0, concat_axis=0, tiled=True, axis_index_groups=[NEAR_ORDER]
    )
    both = both.reshape(zb * yb * own, -1)
    factors = both[:, :half]
    split = half + ys * rows

    def product(part):
        out = lax.dot_general(
            part, factors, (((part.ndim - 2,), (0,)), ((), ())),
            preferred_element_type=jnp.float32,
        )
        return out.astype(jnp.bfloat16).reshape(ys, rows, half)

    def reduce_y(block):
        block = lax.all_to_all(block, ALONG, split_axis=0, concat_axis=0, tiled=True)
        block = block.astype(jnp.float32).reshape([size[a] for a in ALONG] + [rows, half])
        where = ALONG.index("y0")
        return jnp.sum(block, axis=tuple(i for i in range(3) if i != where))

    pairs = [(z, zb + PARTNER[z]) for z in range(zb)] + [(zb + PARTNER[z], z) for z in range(zb)]
    far, near = lax.optimization_barrier((product(both[:, half:split]), both[:, split:]))
    near = product(lax.all_gather(near, "core"))
    far = reduce_y(far).astype(jnp.bfloat16)
    far, near = lax.optimization_barrier((far, near))
    far = lax.ppermute(far, ("za", "zb"), pairs)
    update = reduce_y(near) + far.astype(jnp.float32)
    update = update.transpose(1, 0, 2).reshape(rows, cols)
    return weight + 3.0 / math.sqrt(members) * update


def solution(mesh):
    pop, col = mesh.devices.shape
    fine = Mesh(
        mesh.devices.reshape(2, 2, YB, 6 // ZB, ZB, col // 2, 2),
        ("y2", "y1", "y0", "za", "zb", "plane", "core"),
    )
    pop, col = ("y2", "y1", "y0", "za", "zb"), ("plane", "core")
    in_specs = (P(pop, col), P(None, pop), P(pop, col), P(pop))
    out_specs = P(pop, col)
    return jax.shard_map(body, mesh=fine, in_specs=in_specs, out_specs=out_specs, check_vma=False)
```

```python
import math

import jax
import jax.numpy as jnp
from jax import lax
from jax.sharding import Mesh, PartitionSpec as P

YB, ZB = 2, 3
NEAR = ("y0", "zb")
NEAR_ORDER = (1, 2, 0, 4, 5, 3)
PARTNER = (0, 1, 2)
ALONG = ("y1", "y2", "y0")


def body(weight, row_factors, col_factors, fitness_ranks):
    size = {a: lax.axis_size(a) for a in ("y2", "y1", "y0", "za", "zb")}
    yb, za, zb = size["y0"], size["za"], size["zb"]
    ys = size["y2"] * size["y1"] * yb
    members = fitness_ranks.shape[0] * ys * za * zb
    rows, cols = weight.shape
    own = fitness_ranks.shape[0]
    half = cols // yb
    shaped = fitness_ranks.astype(jnp.float32) / (members - 1) - 0.5
    scaled = (shaped[:, None] * col_factors.astype(jnp.float32)).astype(jnp.bfloat16)
    scaled = scaled.reshape(own, yb, half).transpose(1, 0, 2)
    scaled = jnp.broadcast_to(scaled, (zb, yb, own, half))
    here = lax.axis_index("za")
    part = row_factors.reshape(size["y2"], size["y1"], yb, za, zb, rows, own)
    there = lax.dynamic_index_in_dim(part, 1 - here, 3, False)
    there = jnp.stack([there[:, :, :, z] for z in PARTNER], axis=3)
    part = lax.dynamic_index_in_dim(part, here, 3, False)
    part = lax.dynamic_index_in_dim(part, lax.axis_index("core"), 1, False)
    packed = []
    there = there.swapaxes(0, 1)
    for rows_of in (there.reshape(ys, zb, rows, own), part.reshape(ys // 2, zb, rows, own)):
        rows_of = jnp.stack([rows_of[:, z] for z in NEAR_ORDER[:zb]])
        packed.append(rows_of.transpose(0, 3, 1, 2).reshape(zb, 1, own, -1))
    part = jnp.concatenate(packed, axis=3)
    part = jnp.broadcast_to(part, (zb, yb, own, part.shape[3]))
    both = jnp.concatenate([scaled, part], axis=3)
    if NEAR[0] == "y0":
        both = both.transpose(1, 0, 2, 3)
    both = both.reshape(zb * yb, own, -1)
    both = lax.all_to_all(
        both, NEAR, split_axis=0, concat_axis=0, tiled=True, axis_index_groups=[NEAR_ORDER]
    )
    both = both.reshape(zb * yb * own, -1)
    factors = both[:, :half]
    split = half + ys * rows

    def product(part):
        out = lax.dot_general(
            part, factors, (((part.ndim - 2,), (0,)), ((), ())),
            preferred_element_type=jnp.float32,
        )
        return out.astype(jnp.bfloat16).reshape(ys, rows, half)

    def reduce_y(block):
        block = lax.all_to_all(block, ALONG, split_axis=0, concat_axis=0, tiled=True)
        block = block.astype(jnp.float32).reshape([size[a] for a in ALONG] + [rows, half])
        where = ALONG.index("y0")
        return jnp.sum(block, axis=tuple(i for i in range(3) if i != where))

    back = [(zb + PARTNER[z], z) for z in range(zb)]
    far, near = lax.optimization_barrier((product(both[:, half:split]), both[:, split:]))
    near = product(lax.all_gather(near, "core"))
    far = reduce_y(far).astype(jnp.bfloat16)
    first = lax.ppermute(far, ("za", "zb"), back)
    far, near = lax.optimization_barrier((far, near))
    second = lax.ppermute(far, ("za", "zb"), [(b, a) for a, b in back])
    update = reduce_y(near) + (first.astype(jnp.float32) + second.astype(jnp.float32))
    update = update.transpose(1, 0, 2).reshape(rows, cols)
    return weight + 3.0 / math.sqrt(members) * update


def solution(mesh):
    pop, col = mesh.devices.shape
    fine = Mesh(
        mesh.devices.reshape(2, 2, YB, 6 // ZB, ZB, col // 2, 2),
        ("y2", "y1", "y0", "za", "zb", "plane", "core"),
    )
    pop, col = ("y2", "y1", "y0", "za", "zb"), ("plane", "core")
    in_specs = (P(pop, col), P(None, pop), P(pop, col), P(pop))
    out_specs = P(pop, col)
    return jax.shard_map(body, mesh=fine, in_specs=in_specs, out_specs=out_specs, check_vma=False)
```
